32 devices in a mesh: dom: 8 (over z, y), feat: 4 (over x, core).
Axes of the slice: x: 2, y: 2, z: 4, core: 2. Of those that a mesh axis runs over, the one named last changes fastest.
Arguments:
- latents: bfloat16 [16384, 1024], P('dom', 'feat'), may hold values from -6 to 6
- w_src: bfloat16 [1024, 1024], P(None, 'feat'), may hold values from -0.1875 to 0.1875
- w_dst: bfloat16 [1024, 1024], P(None, 'feat'), may hold values from -0.1875 to 0.1875
- w_edge_out: bfloat16 [1024, 1024], P('feat'), may hold values from -0.1875 to 0.1875
- w_node_in: bfloat16 [2048, 1024], P(None, 'feat'), may hold values from -0.125 to 0.125
- w_node_out: bfloat16 [1024, 1024], P('feat'), may hold values from -0.1875 to 0.1875
- norm_gain: float32 [1024], P('feat'), may hold values from 0.5 to 2
- norm_bias: float32 [1024], P('feat'), may hold values from -3 to 3
- src_tile: int32 [768, 128], P('dom'), may hold values from 0 to 47, as said below
- dst_tile: int32 [8, 96], P('dom'), may hold values from 0 to 15
- src_off: int32 [768, 128], P('dom'), may hold values from 0 to 127
- dst_off: int32 [768, 128], P('dom'), may hold values from 0 to 127
- edge_count: int32 [8], P('dom'), may hold values from 24 to 96, as said below
- send_tiles: int32 [8, 4, 4], P('dom'), may hold values from 0 to 15
Outputs:
- new_latents: bfloat16 [16384, 1024], P('dom', 'feat')
The draws below stay inside these ranges and needn't reach their ends.
Inputs may be any that keep to these rules, and one draw needn't show every extreme that they name: `src_tile`: in each partition's rows, every edge of edge tile e < 16 has sender tile 16 + e (halo slot e); every edge of edge tiles 16 to 23 has a coarse tile (32 and up), each edge its own; all later edges have sender tiles below 32. `edge_count`: skewed over partitions; some partition has all 96 edge tiles live.
All inputs are finite; a program needn't handle non-finite values.
Results may differ from the reference program's by a relative error of at most 0.013.
Values may be sent and summed in bfloat16 or wider, within the bound.
A program may use at most 128 MiB of HBM per device.

```python
import math
import jax
import jax.numpy as jnp
from jax import lax

D = 1024
TILE = 128
NT = 16
CT = 2
CE = 8
W = 2
NB = 4
ET = 96
NODES = 16384
N_DOM = 8
N_FEAT = 4


def draw_src_tile(key, part):
    key = jax.random.fold_in(key, 11)
    key_one, key_two = jax.random.split(key)
    halo_count = 2 * W * NB
    halo_ids = jnp.broadcast_to((NT + jnp.arange(halo_count, dtype=jnp.int32))[None, :, None], (N_DOM, halo_count, TILE))
    coarse_ids = NT + halo_count + jax.random.randint(key_one, (N_DOM, CE, TILE), 0, N_DOM * CT)
    other_ids = jax.random.randint(key_two, (N_DOM, ET - halo_count - CE, TILE), 0, NT + halo_count)
    coarse_ids = coarse_ids.at[0, 0, 0].set(NT + halo_count + N_DOM * CT - 1)
    other_ids = other_ids.at[0, 0, 0].set(0)
    whole = jnp.concatenate([halo_ids.astype(jnp.int32), coarse_ids.astype(jnp.int32), other_ids.astype(jnp.int32)], 1)
    return whole.reshape(N_DOM * ET, TILE).astype(jnp.int32)


def draw_edge_count(key, part):
    key = jax.random.fold_in(key, 12)
    key_one, key_two, key_three = jax.random.split(key, 3)
    floor_count = 2 * W * NB + CE
    span_count = ET - floor_count
    first_part = jax.random.randint(key_one, (N_DOM,), 0, span_count + 1)
    second_part = jax.random.randint(key_two, (N_DOM,), 0, span_count + 1)
    counts = floor_count + first_part * second_part // max(span_count, 1)
    busiest = jax.random.randint(key_three, (), 0, N_DOM)
    counts = jnp.where(jnp.arange(N_DOM) == busiest, ET, counts)
    return counts.astype(jnp.int32)


def place_ends(drawn, own_key, smallest, top_value):
    index_at = [jax.random.randint(jax.random.fold_in(own_key, axis), (), 0, length) for axis, length in enumerate(drawn.shape)]
    main_axis = drawn.shape.index(max(drawn.shape))
    neighbour = index_at[:main_axis] + [(index_at[main_axis] + 1) % drawn.shape[main_axis]] + index_at[main_axis + 1:]
    return drawn.at[tuple(index_at)].set(smallest).at[tuple(neighbour)].set(top_value)


def steps_of(key, dims, cuts, low, top_value):
    level, own = 1.0, jax.random.fold_in(key, 6)
    for position, shards_of in cuts:
        draws = jnp.exp(jax.random.uniform(jax.random.fold_in(own, position), (shards_of,), jnp.float32, low / len(cuts), top_value / len(cuts)))
        level = level * jnp.repeat(draws, dims[position] // shards_of).reshape([-1 if axis == position else 1 for axis in range(len(dims))])
    return level


def gaussian(stream_key, extent, deviation, limit, shards=(), kind=jnp.bfloat16):
    result = jax.random.normal(stream_key, extent, jnp.float32) * deviation
    if len(shards) > 0:
        result = steps_of(stream_key, extent, shards, -0.22, 0.18) * result
    return jnp.clip(result, min=-limit, max=limit).astype(kind)


def setup_inputs(seed: int = 0) -> dict:
    seeds = jax.random.split(jax.random.key(seed), 15)
    return {
        "latents": gaussian(seeds[0], (NODES, D), 1.0, 6.0, ((0, 8), (1, 4))),
        "w_src": gaussian(seeds[1], (D, D), D ** -0.5, 0.1875, ((1, 4),)),
        "w_dst": gaussian(seeds[2], (D, D), D ** -0.5, 0.1875, ((1, 4),)),
        "w_edge_out": gaussian(seeds[3], (D, D), D ** -0.5, 0.1875, ((0, 4),)),
        "w_node_in": gaussian(seeds[4], (2 * D, D), (2 * D) ** -0.5, 0.125, ((1, 4),)),
        "w_node_out": gaussian(seeds[5], (D, D), D ** -0.5, 0.1875, ((0, 4),)),
        "norm_gain": jnp.clip(jnp.exp(math.log(2.0) - 1.3862944 * jax.random.uniform(seeds[6], (D,), jnp.float32) ** steps_of(seeds[6], (D,), ((0, 4),), -0.2, 0.2)), 0.5, 2.0),
        "norm_bias": gaussian(seeds[7], (D,), 0.5, 3.0, ((0, 4),), jnp.float32),
        "src_tile": draw_src_tile(jax.random.fold_in(seeds[14], 71), 0),
        "dst_tile": place_ends(jax.random.randint(seeds[9], (N_DOM, ET), 0, NT), jax.random.fold_in(seeds[9], 1), 0, NT - 1).astype(jnp.int32),
        "src_off": place_ends(jax.random.randint(seeds[10], (N_DOM * ET, TILE), 0, TILE), jax.random.fold_in(seeds[10], 1), 0, TILE - 1).astype(jnp.int32),
        "dst_off": place_ends(jax.random.randint(seeds[11], (N_DOM * ET, TILE), 0, TILE), jax.random.fold_in(seeds[11], 1), 0, TILE - 1).astype(jnp.int32),
        "edge_count": draw_edge_count(jax.random.fold_in(seeds[14], 71), 0),
        "send_tiles": place_ends(jax.random.randint(seeds[13], (N_DOM, 2 * W, NB), 0, NT), jax.random.fold_in(seeds[13], 1), 0, NT - 1).astype(jnp.int32),
    }


epsilon = 1e-05

def grouped_sum(left, right):
    group_width = D // N_FEAT
    total = jnp.zeros((left.shape[0], right.shape[1]), jnp.float32)
    for group in range(N_FEAT):
        term = jnp.dot(left[:, group * group_width:(group + 1) * group_width], right[group * group_width:(group + 1) * group_width], preferred_element_type=jnp.float32).astype(jnp.bfloat16)
        term = lax.optimization_barrier(term)
        total = total + term.astype(jnp.float32)
    return total

def reference(latents, w_src, w_dst, w_edge_out, w_node_in, w_node_out, norm_gain, norm_bias, src_tile, dst_tile, src_off, dst_off, edge_count, send_tiles):
    sender = jnp.dot(latents, w_src, preferred_element_type=jnp.float32).astype(jnp.bfloat16)
    receiver = jnp.dot(latents, w_dst, preferred_element_type=jnp.float32).astype(jnp.bfloat16)
    sender_tiles = sender.reshape(N_DOM, NT, TILE, D)
    receiver_rows = receiver.reshape(N_DOM, NT * TILE, D)
    coarse_rows = sender_tiles[:, :CT].reshape(N_DOM * CT * TILE, D)
    offsets = list(range(-W, 0)) + list(range(1, W + 1))
    src_tile_tiles = src_tile.reshape(N_DOM, ET, TILE)
    src_off_tiles = src_off.reshape(N_DOM, ET, TILE)
    dst_off_tiles = dst_off.reshape(N_DOM, ET, TILE)

    def one_part(part_index):
        pieces = [sender_tiles[part_index].reshape(NT * TILE, D)]
        for round_index, offset in enumerate(offsets):
            partner = part_index + offset
            inside_mask = ((partner >= 0) & (partner < N_DOM)).astype(jnp.bfloat16)
            partner_clip = jnp.clip(partner, 0, N_DOM - 1).astype(jnp.int32)
            chosen = sender_tiles[partner_clip][send_tiles[partner_clip, round_index]]
            pieces.append((chosen * inside_mask).reshape(NB * TILE, D))
        pieces.append(coarse_rows)
        src_table = jnp.concatenate(pieces, 0)
        src_index = (src_tile_tiles[part_index] * TILE + src_off_tiles[part_index]).reshape(-1).astype(jnp.int32)
        dst_index = (dst_tile[part_index][:, None] * TILE + dst_off_tiles[part_index]).reshape(-1).astype(jnp.int32)
        sources = src_table[src_index].astype(jnp.float32)
        targets = receiver_rows[part_index][dst_index].astype(jnp.float32)
        live_tiles = (jnp.arange(ET, dtype=jnp.int32) < edge_count[part_index]).astype(jnp.float32)
        live_mask = jnp.repeat(live_tiles, TILE)[:, None]
        message = (jax.nn.silu(sources + targets) * live_mask).astype(jnp.bfloat16)
        summed = jax.ops.segment_sum(message.astype(jnp.float32), dst_index, num_segments=NT * TILE)
        return summed.astype(jnp.bfloat16)
    summed_all = lax.map(one_part, jnp.arange(N_DOM, dtype=jnp.int32)).reshape(N_DOM * NT * TILE, D)
    aggregate = grouped_sum(summed_all, w_edge_out).astype(jnp.bfloat16)
    node_pre = jnp.dot(latents, w_node_in[:D], preferred_element_type=jnp.float32)
    node_pre = node_pre + jnp.dot(aggregate, w_node_in[D:], preferred_element_type=jnp.float32)
    hidden = jax.nn.silu(node_pre).astype(jnp.bfloat16)
    update = grouped_sum(hidden, w_node_out)
    average = lax.optimization_barrier(jnp.mean(update, axis=1, keepdims=True))
    spread = lax.optimization_barrier(jnp.mean(update * update, axis=1, keepdims=True)) - average * average
    normed = (update - average) * lax.rsqrt(spread + epsilon) * norm_gain + norm_bias
    return (latents.astype(jnp.float32) + normed).astype(jnp.bfloat16)
```

```python
import functools

import jax
import jax.numpy as jnp
from jax import lax
from jax.experimental import pallas as pl
from jax.experimental.pallas import tpu as pltpu
from jax.sharding import PartitionSpec as P

TILE = 128
CT = 2
W = 2
MESH = pl.DeviceIdType.MESH
BF = jnp.bfloat16
F32 = jnp.float32
MIB = 1 << 20

epsilon = 1e-05


def swish(v):
    half = 0.5 * v
    return half + half * jnp.tanh(half)


def project_kernel(
    lat_ref,
    ws_ref,
    wd_ref,
    st_ref,
    table_ref,
    recv_ref,
    rows_ref,
    parts,
    held,
    halo,
    own_sem,
    a1_send,
    a1_recv,
    a2_send,
    a2_recv,
    b_send,
    b_recv,
    c_send,
    c_recv,
    h_send,
    h_recv,
):
    nf, nodes, width = parts.shape
    nd = lax.axis_size("dom")
    feat = lax.axis_index("feat")
    dom = lax.axis_index("dom")
    rounds, batch = st_ref.shape[1:]
    chunks = a1_send.shape[0]
    step = nodes // chunks
    x, core = feat // 2, feat % 2
    near = x * 2 + (1 - core)
    far = (1 - x) * 2 + core
    offsets = list(range(-W, 0)) + list(range(1, W + 1))
    coarse_at = nodes + rounds * batch * TILE
    coarse_rows = CT * TILE

    barrier = pltpu.get_barrier_semaphore()
    for peer in (near, far):
        pl.semaphore_signal(barrier, inc=1, device_id={"feat": peer}, device_id_type=MESH)
    for k in range(1, nd):
        pl.semaphore_signal(
            barrier, inc=1, device_id={"dom": lax.rem(dom + k, nd)}, device_id_type=MESH
        )
    pl.semaphore_wait(barrier, nd + 1)

    def first(c, peer, send, recv):
        rows = pl.ds(c * step, step)
        return pltpu.make_async_remote_copy(
            src_ref=lat_ref.at[rows],
            dst_ref=parts.at[feat, rows],
            send_sem=send.at[c],
            recv_sem=recv.at[c],
            device_id={"feat": peer},
            device_id_type=MESH,
        )

    to_far = [first(c, far, a2_send, a2_recv) for c in range(chunks)]
    to_near = [first(c, near, a1_send, a1_recv) for c in range(chunks)]
    onward = []
    for c in range(chunks):
        rows = pl.ds(c * step, step)
        onward.append(
            pltpu.make_async_remote_copy(
                src_ref=parts.at[far, rows],
                dst_ref=parts.at[far, rows],
                send_sem=b_send.at[c],
                recv_sem=b_recv.at[c],
                device_id={"feat": near},
                device_id_type=MESH,
            )
        )
    own = pltpu.make_async_copy(lat_ref, parts.at[feat], own_sem)
    for c in range(chunks):
        to_far[c].start()
    own.start()
    for c in range(chunks):
        to_near[c].start()
    own.wait()

    coarse = []
    for k in range(1, nd):
        coarse.append(
            pltpu.make_async_remote_copy(
                src_ref=table_ref.at[pl.ds(0, coarse_rows)],
                dst_ref=table_ref.at[pl.ds(coarse_at + dom * coarse_rows, coarse_rows)],
                send_sem=c_send.at[k],
                recv_sem=c_recv.at[k],
                device_id={"dom": lax.rem(dom + k, nd)},
                device_id_type=MESH,
            )
        )

    def project(c):
        to_near[c].wait_recv()
        onward[c].wait_recv()
        rows = pl.ds(c * step, step)
        lat = jnp.concatenate([parts[f, rows, :] for f in range(nf)], axis=1)
        sent = jnp.dot(lat, ws_ref[...], preferred_element_type=F32).astype(BF)
        tiles = step // TILE
        held[pl.ds(c * tiles, tiles)] = sent.reshape(tiles, TILE, width)
        table_ref[rows, :] = sent
        recv_ref[rows, :] = jnp.dot(lat, wd_ref[...], preferred_element_type=F32).astype(BF)
        if c == 0:
            for copy in coarse:
                copy.start()
            table_ref[pl.ds(coarse_at + dom * coarse_rows, coarse_rows), :] = sent[:coarse_rows]

    for c in range(chunks):
        to_far[c].wait_recv()
        onward[c].start()
        if c > 0:
            project(c - 1)
    project(chunks - 1)

    spread = []
    for r, offset in enumerate(offsets):
        base = nodes + r * batch * TILE
        for b in range(batch):
            tile = st_ref[0, r, b]
            halo[r, pl.ds(b * TILE, TILE), :] = held[tile]
        target = dom - offset
        copy = pltpu.make_async_remote_copy(
            src_ref=halo.at[r],
            dst_ref=table_ref.at[pl.ds(base, batch * TILE)],
            send_sem=h_send.at[r],
            recv_sem=h_recv.at[r],
            device_id={"dom": lax.rem(target + nd, nd)},
            device_id_type=MESH,
        )
        source = dom + offset
        sends = target >= 0 if offset > 0 else target < nd
        gets = source >= 0 if offset < 0 else source < nd
        lacks = source < 0 if offset < 0 else source >= nd
        spread.append((copy, sends, gets))

        @pl.when(sends)
        def _(copy=copy):
            copy.start()

        @pl.when(lacks)
        def _(base=base):
            table_ref[pl.ds(base, batch * TILE), :] = jnp.zeros((batch * TILE, width), BF)

    share = nodes // nf
    for f in range(nf):
        rows_ref[:, f * width : (f + 1) * width] = parts[f, pl.ds(feat * share, share), :]

    for copy, sends, gets in spread:

        @pl.when(sends)
        def _(copy=copy):
            copy.wait_send()

        @pl.when(gets)
        def _(copy=copy):
            copy.wait_recv()

    for copy in coarse:
        copy.wait_send()
        copy.wait_recv()
    for c in range(chunks):
        to_far[c].wait_send()
        to_near[c].wait_send()
        onward[c].wait_send()


UNROLL = 4


def edge_kernel(
    idx_ref, dst_tile_ref, count_ref, off_ref, table_ref, recv_ref, out_ref, wide, acc, *slots
):
    rows, width = table_ref.shape
    half = width // 2
    block = 8 * TILE

    @pl.loop(0, rows // block)
    def _(i):
        part = table_ref[pl.ds(pl.multiple_of(i * block, block), block), :].astype(F32)
        at = pl.multiple_of(i * (2 * block), 2 * block)
        wide[pl.ds(at, block, stride=2), :] = part[:, :half]
        wide[pl.ds(at + 1, block, stride=2), :] = part[:, half:]

    acc[...] = jnp.zeros_like(acc)
    ids = lax.broadcasted_iota(jnp.int32, (TILE, TILE), 0)
    count = count_ref[0]

    @pl.loop(0, (count + UNROLL - 1) // UNROLL)
    def _(i):
        for u in range(UNROLL):
            e = i * UNROLL + u
            slot = slots[u]
            for n in range(TILE):
                slot[pl.ds(2 * n, 2), :] = wide[pl.ds(idx_ref[e, n], 2), :]
        for u in range(UNROLL):
            e = i * UNROLL + u
            slot = slots[u]
            live = (e < count).astype(F32)
            node = pl.ds(pl.multiple_of(dst_tile_ref[0, e] * TILE, TILE), TILE)
            scatter = (ids == off_ref[pl.ds(e, 1), :]).astype(F32).astype(BF)
            target = lax.dot_general(
                scatter, recv_ref[node, :], (((0,), (0,)), ((), ())), preferred_element_type=F32
            )
            source = jnp.concatenate(
                [slot[pl.ds(0, TILE, stride=2), :], slot[pl.ds(1, TILE, stride=2), :]], axis=1
            )
            message = (swish(source + target) * live).astype(BF)
            acc[node, :] += jnp.dot(scatter, message, preferred_element_type=F32)

    out_ref[...] = acc[...].astype(BF)


def node_kernel(
    summed_ref,
    rows_ref,
    we_hbm,
    wi_hbm,
    wo_hbm,
    gain_ref,
    bias_ref,
    out_ref,
    we,
    wi,
    wo,
    taken,
    given,
    load_sem,
    keep_sem,
    in_send,
    in_recv,
    out_send,
    out_recv,
):
    nf, share, width = taken.shape
    full = nf * width
    feat = lax.axis_index("feat")
    chunks = keep_sem.shape[0]
    step = share // chunks

    barrier = pltpu.get_barrier_semaphore()
    for k in range(1, nf):
        pl.semaphore_signal(
            barrier, inc=1, device_id={"feat": lax.rem(feat + k, nf)}, device_id_type=MESH
        )
    loads = [
        pltpu.make_async_copy(src, dst, load_sem.at[i])
        for i, (src, dst) in enumerate(((wi_hbm, wi), (we_hbm, we), (wo_hbm, wo)))
    ]
    pl.semaphore_wait(barrier, nf - 1)

    ins = {}
    for c in range(chunks):
        for k in (2, 1, 3):
            peer = lax.rem(feat + k, nf)
            ins[c, k] = pltpu.make_async_remote_copy(
                src_ref=summed_ref.at[pl.ds(peer * share + c * step, step)],
                dst_ref=taken.at[feat, pl.ds(c * step, step)],
                send_sem=in_send.at[c, k],
                recv_sem=in_recv.at[c, k],
                device_id={"feat": peer},
                device_id_type=MESH,
            )
            ins[c, k].start()
    for load in loads:
        load.start()
    taken[feat] = summed_ref[pl.ds(feat * share, share), :]
    for load in loads:
        load.wait()

    outs = []
    keeps = []
    for c in range(chunks):
        rows = pl.ds(c * step, step)
        lat = rows_ref[rows, :]
        first = [
            jnp.dot(lat, wi[f, :full, :], preferred_element_type=F32) for f in range(nf)
        ]
        for k in (2, 1, 3):
            ins[c, k].wait_recv()
        total = jnp.zeros((step, full), F32)
        for f in range(nf):
            term = jnp.dot(
                taken[f, rows, :], we[f * width : (f + 1) * width, :], preferred_element_type=F32
            )
            total = total + term.astype(BF).astype(F32)
        aggregate = total.astype(BF)
        update = jnp.zeros((step, full), F32)
        for f in range(nf):
            pre = first[f] + jnp.dot(aggregate, wi[f, full:, :], preferred_element_type=F32)
            hidden = swish(pre).astype(BF)
            term = jnp.dot(hidden, wo[f * width : (f + 1) * width, :], preferred_element_type=F32)
            update = update + term.astype(BF).astype(F32)
        average = jnp.sum(update, axis=1, keepdims=True) / full
        spread = jnp.sum(update * update, axis=1, keepdims=True) / full - average * average
        normed = (update - average) * lax.rsqrt(spread + epsilon) * gain_ref[...] + bias_ref[...]
        result = (lat.astype(F32) + normed).astype(BF)
        for f in range(nf):
            given[f, rows, :] = result[:, f * width : (f + 1) * width]
        place = pl.ds(feat * share + c * step, step)
        for k in (2, 1, 3):
            peer = lax.rem(feat + k, nf)
            copy = pltpu.make_async_remote_copy(
                src_ref=given.at[peer, rows],
                dst_ref=out_ref.at[place],
                send_sem=out_send.at[c, k],
                recv_sem=out_recv.at[c, k],
                device_id={"feat": peer},
                device_id_type=MESH,
            )
            copy.start()
            outs.append(copy)
        keep = pltpu.make_async_copy(given.at[feat, rows], out_ref.at[place], keep_sem.at[c])
        keep.start()
        keeps.append(keep)
    for keep in keeps:
        keep.wait()
    for copy in outs:
        copy.wait_send()
        copy.wait_recv()
    for copy in ins.values():
        copy.wait_send()


def vmem():
    return pl.BlockSpec(memory_space=pltpu.VMEM)


def smem():
    return pl.BlockSpec(memory_space=pltpu.SMEM)


def hbm():
    return pl.BlockSpec(memory_space=pl.ANY)


def dma(*shape):
    return pltpu.SemaphoreType.DMA(shape)


def body(
    latents,
    w_src,
    w_dst,
    w_edge_out,
    w_node_in,
    w_node_out,
    norm_gain,
    norm_bias,
    src_tile,
    dst_tile,
    src_off,
    dst_off,
    edge_count,
    send_tiles,
):
    nodes, width = latents.shape
    full = w_src.shape[0]
    nf = lax.axis_size("feat")
    nd = lax.axis_size("dom")
    rounds, batch = send_tiles.shape[1:]
    share = nodes // nf
    table_rows = nodes + rounds * batch * TILE + nd * CT * TILE
    edge_tiles = src_tile.shape[0]
    chunks = 8

    we = lax.all_gather(w_edge_out, "feat", axis=0, tiled=True)
    wi = lax.all_gather(w_node_in, "feat", axis=0)
    wo = lax.all_gather(w_node_out, "feat", axis=0, tiled=True)
    norm = lax.all_gather(jnp.stack([norm_gain, norm_bias]), "feat", axis=1, tiled=True)

    table, received, rows = pl.pallas_call(
        project_kernel,
        out_shape=(
            jax.ShapeDtypeStruct((table_rows, width), BF),
            jax.ShapeDtypeStruct((nodes, width), BF),
            jax.ShapeDtypeStruct((share, full), BF),
        ),
        in_specs=[hbm(), vmem(), vmem(), smem()],
        out_specs=(vmem(), vmem(), vmem()),
        scratch_shapes=[
            pltpu.VMEM((nf, nodes, width), BF),
            pltpu.VMEM((nodes // TILE, TILE, width), BF),
            pltpu.VMEM((rounds, batch * TILE, width), BF),
            pltpu.SemaphoreType.DMA,
            *[dma(chunks) for _ in range(6)],
            dma(nd),
            dma(nd),
            dma(rounds),
            dma(rounds),
        ],
        compiler_params=pltpu.CompilerParams(
            collective_id=0, has_side_effects=True, vmem_limit_bytes=40 * MIB
        ),
        cost_estimate=pl.CostEstimate(
            flops=4 * nodes * full * width, bytes_accessed=100 * MIB, transcendentals=0
        ),
        name="project",
    )(latents, w_src, w_dst, send_tiles)

    index = (src_tile * TILE + src_off) * 2
    summed = pl.pallas_call(
        edge_kernel,
        out_shape=jax.ShapeDtypeStruct((nodes, width), BF),
        in_specs=[smem(), smem(), smem(), vmem(), vmem(), vmem()],
        out_specs=vmem(),
        scratch_shapes=[
            pltpu.VMEM((2 * table_rows, width // 2), F32),
            pltpu.VMEM((nodes, width), F32),
            *[pltpu.VMEM((2 * TILE, width // 2), F32) for _ in range(UNROLL)],
        ],
        compiler_params=pltpu.CompilerParams(vmem_limit_bytes=56 * MIB),
        cost_estimate=pl.CostEstimate(
            flops=4 * edge_tiles * TILE * TILE * width,
            bytes_accessed=100 * MIB,
            transcendentals=edge_tiles * TILE * width,
        ),
        name="edges",
    )(index, dst_tile, edge_count, dst_off, table, received)

    return pl.pallas_call(
        node_kernel,
        out_shape=jax.ShapeDtypeStruct((nodes, width), BF),
        in_specs=[vmem(), vmem(), hbm(), hbm(), hbm(), vmem(), vmem()],
        out_specs=hbm(),
        scratch_shapes=[
            pltpu.VMEM((full, full), BF),
            pltpu.VMEM((nf, 2 * full, width), BF),
            pltpu.VMEM((full, full), BF),
            pltpu.VMEM((nf, share, width), BF),
            pltpu.VMEM((nf, share, width), BF),
            dma(3),
            dma(4),
            dma(4, nf),
            dma(4, nf),
            dma(4, nf),
            dma(4, nf),
        ],
        compiler_params=pltpu.CompilerParams(
            collective_id=1, has_side_effects=True, vmem_limit_bytes=40 * MIB
        ),
        cost_estimate=pl.CostEstimate(
            flops=8 * share * full * full, bytes_accessed=60 * MIB, transcendentals=share * full
        ),
        name="nodes",
    )(summed, rows, we, wi, wo, norm[0:1], norm[1:2])


def solution(mesh):
    in_specs = (
        P("dom", "feat"),
        P(None, "feat"),
        P(None, "feat"),
        P("feat", None),
        P(None, "feat"),
        P("feat", None),
        P("feat"),
        P("feat"),
        P("dom", None),
        P("dom", None),
        P("dom", None),
        P("dom", None),
        P("dom"),
        P("dom", None, None),
    )
    out_specs = P("dom", "feat")
    return jax.shard_map(body, mesh=mesh, in_specs=in_specs, out_specs=out_specs, check_vma=False)
```

```python
import functools

import jax
import jax.numpy as jnp
from jax import lax
from jax.experimental import pallas as pl
from jax.experimental.pallas import tpu as pltpu
from jax.sharding import PartitionSpec as P

TILE = 128
CT = 2
W = 2
MESH = pl.DeviceIdType.MESH
BF = jnp.bfloat16
F32 = jnp.float32
MIB = 1 << 20

epsilon = 1e-05


def swish(v):
    half = 0.5 * v
    return half + half * jnp.tanh(half)


def project_kernel(
    lat_ref,
    ws_hbm,
    wd_hbm,
    st_ref,
    norm_ref,
    we_own,
    wi_own,
    wo_own,
    table_ref,
    recv_ref,
    rows_ref,
    norm_all,
    we_all,
    wi_all,
    wo_all,
    ws_ref,
    wd_ref,
    parts,
    held,
    halo,
    own_sem,
    a1_send,
    a1_recv,
    a2_send,
    a2_recv,
    b_send,
    b_recv,
    c_send,
    c_recv,
    h_send,
    h_recv,
    n_send,
    n_recv,
    near_send,
    near_recv,
    far_send,
    far_recv,
    side_send,
    side_recv,
    pass_send,
    pass_recv,
    load_sem,
):
    nf, nodes, width = parts.shape
    nd = lax.axis_size("dom")
    feat = lax.axis_index("feat")
    dom = lax.axis_index("dom")
    rounds, batch = st_ref.shape[1:]
    chunks = a1_send.shape[0]
    step = nodes // chunks
    x, core = feat // 2, feat % 2
    near = x * 2 + (1 - core)
    far = (1 - x) * 2 + core
    offsets = list(range(-W, 0)) + list(range(1, W + 1))
    coarse_at = nodes + rounds * batch * TILE
    coarse_rows = CT * TILE

    barrier = pltpu.get_barrier_semaphore()
    for peer in (near, far):
        pl.semaphore_signal(barrier, inc=1, device_id={"feat": peer}, device_id_type=MESH)
    for k in range(1, nd):
        pl.semaphore_signal(
            barrier, inc=1, device_id={"dom": lax.rem(dom + k, nd)}, device_id_type=MESH
        )
    pl.semaphore_wait(barrier, nd + 1)

    def first(c, peer, send, recv):
        rows = pl.ds(c * step, step)
        return pltpu.make_async_remote_copy(
            src_ref=lat_ref.at[rows],
            dst_ref=parts.at[feat, rows],
            send_sem=send.at[c],
            recv_sem=recv.at[c],
            device_id={"feat": peer},
            device_id_type=MESH,
        )

    to_far = [first(c, far, a2_send, a2_recv) for c in range(chunks)]
    to_near = [first(c, near, a1_send, a1_recv) for c in range(chunks)]
    onward = []
    for c in range(chunks):
        rows = pl.ds(c * step, step)
        onward.append(
            pltpu.make_async_remote_copy(
                src_ref=parts.at[far, rows],
                dst_ref=parts.at[far, rows],
                send_sem=b_send.at[c],
                recv_sem=b_recv.at[c],
                device_id={"feat": near},
                device_id_type=MESH,
            )
        )
    own = pltpu.make_async_copy(lat_ref, parts.at[feat], own_sem)
    loads = [
        pltpu.make_async_copy(src, dst, load_sem.at[i])
        for i, (src, dst) in enumerate(
            (
                (ws_hbm, ws_ref),
                (wd_hbm, wd_ref),
                (we_own, we_all.at[feat]),
                (wi_own, wi_all.at[feat]),
                (wo_own, wo_all.at[feat]),
            )
        )
    ]

    def remote(src, dst, send, recv, i, peer):
        return pltpu.make_async_remote_copy(
            src_ref=src,
            dst_ref=dst,
            send_sem=send.at[i],
            recv_sem=recv.at[i],
            device_id=peer,
            device_id_type=MESH,
        )

    side = lax.rem(dom, 2)
    beside = {"dom": dom + 1 - 2 * side}

    def pieces(half):
        found = []
        for src, dst, count in ((we_own, we_all, 1), (wo_own, wo_all, 1), (wi_own, wi_all, 2)):
            size = src.shape[0] // (2 * count)
            for i in range(count):
                found.append((src, dst, pl.ds(half * (size * count) + i * size, size)))
        return found

    mine, other = pieces(side), pieces(1 - side)
    count = len(mine)
    weights_near = [
        remote(src, dst.at[feat], near_send, near_recv, i, {"feat": near})
        for i, (src, dst) in enumerate(((we_own, we_all), (wi_own, wi_all), (wo_own, wo_all)))
    ]
    weights_far = [
        remote(src.at[at], dst.at[feat, at], far_send, far_recv, i, {"feat": far})
        for i, (src, dst, at) in enumerate(mine)
    ]
    weights_side = [
        remote(dst.at[far, at], dst.at[far, at], side_send, side_recv, i, beside)
        for i, (src, dst, at) in enumerate(mine)
    ]
    weights_pass = [
        remote(dst.at[far, at], dst.at[far, at], pass_send, pass_recv, i, {"feat": near})
        for i, (src, dst, at) in enumerate(mine + other)
    ]
    norms = [
        remote(norm_ref, norm_all.at[feat], n_send, n_recv, 0, {"feat": far}),
        remote(norm_ref, norm_all.at[feat], n_send, n_recv, 1, {"feat": near}),
        remote(norm_all.at[far], norm_all.at[far], n_send, n_recv, 2, {"feat": near}),
    ]
    norms[0].start()
    norms[1].start()
    norm_all[feat] = norm_ref[...]
    for c in range(chunks):
        to_far[c].start()
    own.start()
    for c in range(chunks):
        to_near[c].start()
    for load in loads:
        load.start()
    own.wait()
    loads[0].wait()
    loads[1].wait()

    coarse = []
    for k in range(1, nd):
        coarse.append(
            pltpu.make_async_remote_copy(
                src_ref=table_ref.at[pl.ds(0, coarse_rows)],
                dst_ref=table_ref.at[pl.ds(coarse_at + dom * coarse_rows, coarse_rows)],
                send_sem=c_send.at[k],
                recv_sem=c_recv.at[k],
                device_id={"dom": lax.rem(dom + k, nd)},
                device_id_type=MESH,
            )
        )

    def project(c):
        to_near[c].wait_recv()
        onward[c].wait_recv()
        rows = pl.ds(c * step, step)
        lat = jnp.concatenate([parts[f, rows, :] for f in range(nf)], axis=1)
        sent = jnp.dot(lat, ws_ref[...], preferred_element_type=F32).astype(BF)
        tiles = step // TILE
        held[pl.ds(c * tiles, tiles)] = sent.reshape(tiles, TILE, width)
        table_ref[rows, :] = sent
        recv_ref[rows, :] = jnp.dot(lat, wd_ref[...], preferred_element_type=F32).astype(BF)
        if c == 0:
            for copy in coarse:
                copy.start()
            table_ref[pl.ds(coarse_at + dom * coarse_rows, coarse_rows), :] = sent[:coarse_rows]

    for c in range(chunks):
        to_far[c].wait_recv()
        onward[c].start()
        if c == chunks - 2:
            for copy in weights_far:
                copy.start()
        if c > 0:
            project(c - 1)
    project(chunks - 1)

    spread = []
    for r, offset in enumerate(offsets):
        base = nodes + r * batch * TILE
        for b in range(batch):
            tile = st_ref[0, r, b]
            halo[r, pl.ds(b * TILE, TILE), :] = held[tile]
        target = dom - offset
        copy = pltpu.make_async_remote_copy(
            src_ref=halo.at[r],
            dst_ref=table_ref.at[pl.ds(base, batch * TILE)],
            send_sem=h_send.at[r],
            recv_sem=h_recv.at[r],
            device_id={"dom": lax.rem(target + nd, nd)},
            device_id_type=MESH,
        )
        source = dom + offset
        sends = target >= 0 if offset > 0 else target < nd
        gets = source >= 0 if offset < 0 else source < nd
        lacks = source < 0 if offset < 0 else source >= nd
        spread.append((copy, sends, gets))

        @pl.when(sends)
        def _(copy=copy):
            copy.start()

        @pl.when(lacks)
        def _(base=base):
            table_ref[pl.ds(base, batch * TILE), :] = jnp.zeros((batch * TILE, width), BF)

    for copy in weights_near:
        copy.start()
    norms[0].wait_recv()
    norms[2].start()
    share = nodes // nf
    for f in range(nf):
        rows_ref[:, f * width : (f + 1) * width] = parts[f, pl.ds(feat * share, share), :]

    for i in range(count):
        weights_far[i].wait_recv()
        weights_side[i].start()
        weights_pass[i].start()
    for i in range(count):
        weights_side[i].wait_recv()
        weights_pass[count + i].start()

    for copy, sends, gets in spread:

        @pl.when(sends)
        def _(copy=copy):
            copy.wait_send()

        @pl.when(gets)
        def _(copy=copy):
            copy.wait_recv()

    for copy in coarse:
        copy.wait_send()
        copy.wait_recv()
    for c in range(chunks):
        to_far[c].wait_send()
        to_near[c].wait_send()
        onward[c].wait_send()
    for copy in weights_near + weights_pass + norms[1:]:
        copy.wait_send()
        copy.wait_recv()
    for copy in weights_far + weights_side + norms[:1]:
        copy.wait_send()
    for load in loads[2:]:
        load.wait()


UNROLL = 4


def edge_kernel(
    idx_ref,
    dst_tile_ref,
    count_ref,
    off_ref,
    table_hbm,
    recv_hbm,
    out_ref,
    table_ref,
    recv_ref,
    wide,
    acc,
    sems,
    *slots,
):
    rows, width = table_ref.shape
    half = width // 2
    block = 8 * TILE

    loads = []
    for i in range(rows // block):
        at = pl.ds(i * block, block)
        loads.append(pltpu.make_async_copy(table_hbm.at[at], table_ref.at[at], sems.at[i]))
    loads.append(pltpu.make_async_copy(recv_hbm, recv_ref, sems.at[rows // block]))
    for load in loads:
        load.start()
    acc[...] = jnp.zeros_like(acc)
    for i in range(rows // block):
        loads[i].wait()
        part = table_ref[pl.ds(i * block, block), :].astype(F32)
        wide[pl.ds(2 * i * block, block, stride=2), :] = part[:, :half]
        wide[pl.ds(2 * i * block + 1, block, stride=2), :] = part[:, half:]
    loads[-1].wait()
    ids = lax.broadcasted_iota(jnp.int32, (TILE, TILE), 0)
    count = count_ref[0]

    @pl.loop(0, (count + UNROLL - 1) // UNROLL)
    def _(i):
        for u in range(UNROLL):
            e = i * UNROLL + u
            slot = slots[u]
            for n in range(TILE):
                slot[pl.ds(2 * n, 2), :] = wide[pl.ds(idx_ref[e, n], 2), :]
        for u in range(UNROLL):
            e = i * UNROLL + u
            slot = slots[u]
            live = (e < count).astype(F32)
            node = pl.ds(pl.multiple_of(dst_tile_ref[0, e] * TILE, TILE), TILE)
            scatter = (ids == off_ref[pl.ds(e, 1), :]).astype(F32).astype(BF)
            target = lax.dot_general(
                scatter, recv_ref[node, :], (((0,), (0,)), ((), ())), preferred_element_type=F32
            )
            source = jnp.concatenate(
                [slot[pl.ds(0, TILE, stride=2), :], slot[pl.ds(1, TILE, stride=2), :]], axis=1
            )
            message = (swish(source + target) * live).astype(BF)
            acc[node, :] += jnp.dot(scatter, message, preferred_element_type=F32)

    out_ref[...] = acc[...].astype(BF)


def node_kernel(
    summed_ref,
    rows_hbm,
    we_hbm,
    wi_hbm,
    wo_hbm,
    norm_ref,
    out_ref,
    rows_ref,
    we,
    wi,
    wo,
    taken,
    given,
    load_sem,
    keep_sem,
    in_send,
    in_recv,
    out_send,
    out_recv,
):
    nf, share, width = taken.shape
    full = nf * width
    feat = lax.axis_index("feat")
    chunks = keep_sem.shape[0]
    step = share // chunks

    barrier = pltpu.get_barrier_semaphore()
    for k in range(1, nf):
        pl.semaphore_signal(
            barrier, inc=1, device_id={"feat": lax.rem(feat + k, nf)}, device_id_type=MESH
        )
    loads = [
        pltpu.make_async_copy(src, dst, load_sem.at[i])
        for i, (src, dst) in enumerate(
            (
                (rows_hbm, rows_ref),
                (wi_hbm, wi),
                (summed_ref.at[pl.ds(feat * share, share)], taken.at[feat]),
                (we_hbm, we),
                (wo_hbm, wo),
            )
        )
    ]
    pl.semaphore_wait(barrier, nf - 1)

    ins = {}
    for c in range(chunks):
        for k in (2, 1, 3):
            peer = lax.rem(feat + k, nf)
            ins[c, k] = pltpu.make_async_remote_copy(
                src_ref=summed_ref.at[pl.ds(peer * share + c * step, step)],
                dst_ref=taken.at[feat, pl.ds(c * step, step)],
                send_sem=in_send.at[c, k],
                recv_sem=in_recv.at[c, k],
                device_id={"feat": peer},
                device_id_type=MESH,
            )
            ins[c, k].start()
    for load in loads:
        load.start()
    gain = jnp.concatenate([norm_ref[f, 0:1, :] for f in range(nf)], axis=1)
    bias = jnp.concatenate([norm_ref[f, 1:2, :] for f in range(nf)], axis=1)
    loads[0].wait()
    loads[1].wait()

    outs = []
    keeps = []
    for c in range(chunks):
        rows = pl.ds(c * step, step)
        lat = rows_ref[rows, :]
        first = [
            jnp.dot(lat, wi[f, :full, :], preferred_element_type=F32) for f in range(nf)
        ]
        for k in (2, 1, 3):
            ins[c, k].wait_recv()
        if c == 0:
            for load in loads[2:]:
                load.wait()
        total = jnp.zeros((step, full), F32)
        for f in range(nf):
            term = jnp.dot(
                taken[f, rows, :], we[f], preferred_element_type=F32
            )
            total = total + term.astype(BF).astype(F32)
        aggregate = total.astype(BF)
        update = jnp.zeros((step, full), F32)
        for f in range(nf):
            pre = first[f] + jnp.dot(aggregate, wi[f, full:, :], preferred_element_type=F32)
            hidden = swish(pre).astype(BF)
            term = jnp.dot(hidden, wo[f], preferred_element_type=F32)
            update = update + term.astype(BF).astype(F32)
        average = jnp.sum(update, axis=1, keepdims=True) / full
        spread = jnp.sum(update * update, axis=1, keepdims=True) / full - average * average
        normed = (update - average) * lax.rsqrt(spread + epsilon) * gain + bias
        result = (lat.astype(F32) + normed).astype(BF)
        for f in range(nf):
            given[f, rows, :] = result[:, f * width : (f + 1) * width]
        place = pl.ds(feat * share + c * step, step)
        for k in (2, 1, 3):
            peer = lax.rem(feat + k, nf)
            copy = pltpu.make_async_remote_copy(
                src_ref=given.at[peer, rows],
                dst_ref=out_ref.at[place],
                send_sem=out_send.at[c, k],
                recv_sem=out_recv.at[c, k],
                device_id={"feat": peer},
                device_id_type=MESH,
            )
            copy.start()
            outs.append(copy)
        keep = pltpu.make_async_copy(given.at[feat, rows], out_ref.at[place], keep_sem.at[c])
        keep.start()
        keeps.append(keep)
    for keep in keeps:
        keep.wait()
    for copy in outs:
        copy.wait_send()
        copy.wait_recv()
    for copy in ins.values():
        copy.wait_send()


def vmem():
    return pl.BlockSpec(memory_space=pltpu.VMEM)


def smem():
    return pl.BlockSpec(memory_space=pltpu.SMEM)


def hbm():
    return pl.BlockSpec(memory_space=pl.ANY)


def dma(*shape):
    return pltpu.SemaphoreType.DMA(shape)


def body(
    latents,
    w_src,
    w_dst,
    w_edge_out,
    w_node_in,
    w_node_out,
    norm_gain,
    norm_bias,
    src_tile,
    dst_tile,
    src_off,
    dst_off,
    edge_count,
    send_tiles,
):
    nodes, width = latents.shape
    full = w_src.shape[0]
    nf = lax.axis_size("feat")
    nd = lax.axis_size("dom")
    rounds, batch = send_tiles.shape[1:]
    share = nodes // nf
    table_rows = nodes + rounds * batch * TILE + nd * CT * TILE
    edge_tiles = src_tile.shape[0]
    chunks = 8

    norm = jnp.stack([norm_gain, norm_bias])

    table, received, rows, norms, we, wi, wo = pl.pallas_call(
        project_kernel,
        out_shape=(
            jax.ShapeDtypeStruct((table_rows, width), BF),
            jax.ShapeDtypeStruct((nodes, width), BF),
            jax.ShapeDtypeStruct((share, full), BF),
            jax.ShapeDtypeStruct((nf, 2, width), F32),
            jax.ShapeDtypeStruct((nf, width, full), BF),
            jax.ShapeDtypeStruct((nf, 2 * full, width), BF),
            jax.ShapeDtypeStruct((nf, width, full), BF),
        ),
        in_specs=[hbm(), hbm(), hbm(), smem(), vmem(), hbm(), hbm(), hbm()],
        out_specs=(vmem(), vmem(), vmem(), vmem(), hbm(), hbm(), hbm()),
        scratch_shapes=[
            pltpu.VMEM((full, width), BF),
            pltpu.VMEM((full, width), BF),
            pltpu.VMEM((nf, nodes, width), BF),
            pltpu.VMEM((nodes // TILE, TILE, width), BF),
            pltpu.VMEM((rounds, batch * TILE, width), BF),
            pltpu.SemaphoreType.DMA,
            *[dma(chunks) for _ in range(6)],
            dma(nd),
            dma(nd),
            dma(rounds),
            dma(rounds),
            dma(3),
            dma(3),
            dma(3),
            dma(3),
            dma(4),
            dma(4),
            dma(4),
            dma(4),
            dma(8),
            dma(8),
            dma(5),
        ],
        compiler_params=pltpu.CompilerParams(
            collective_id=0, has_side_effects=True, vmem_limit_bytes=40 * MIB
        ),
        cost_estimate=pl.CostEstimate(
            flops=4 * nodes * full * width, bytes_accessed=100 * MIB, transcendentals=0
        ),
        name="project",
    )(latents, w_src, w_dst, send_tiles, norm, w_edge_out, w_node_in, w_node_out)

    index = (src_tile * TILE + src_off) * 2
    summed = pl.pallas_call(
        edge_kernel,
        out_shape=jax.ShapeDtypeStruct((nodes, width), BF),
        in_specs=[smem(), smem(), smem(), vmem(), hbm(), hbm()],
        out_specs=vmem(),
        scratch_shapes=[
            pltpu.VMEM((table_rows, width), BF),
            pltpu.VMEM((nodes, width), BF),
            pltpu.VMEM((2 * table_rows, width // 2), F32),
            pltpu.VMEM((nodes, width), F32),
            dma(table_rows // (8 * TILE) + 1),
            *[pltpu.VMEM((2 * TILE, width // 2), F32) for _ in range(UNROLL)],
        ],
        compiler_params=pltpu.CompilerParams(vmem_limit_bytes=56 * MIB),
        cost_estimate=pl.CostEstimate(
            flops=4 * edge_tiles * TILE * TILE * width,
            bytes_accessed=100 * MIB,
            transcendentals=edge_tiles * TILE * width,
        ),
        name="edges",
    )(index, dst_tile, edge_count, dst_off, table, received)

    return pl.pallas_call(
        node_kernel,
        out_shape=jax.ShapeDtypeStruct((nodes, width), BF),
        in_specs=[hbm(), hbm(), hbm(), hbm(), hbm(), vmem()],
        out_specs=hbm(),
        scratch_shapes=[
            pltpu.VMEM((share, full), BF),
            pltpu.VMEM((nf, width, full), BF),
            pltpu.VMEM((nf, 2 * full, width), BF),
            pltpu.VMEM((nf, width, full), BF),
            pltpu.VMEM((nf, share, width), BF),
            pltpu.VMEM((nf, share, width), BF),
            dma(5),
            dma(4),
            dma(4, nf),
            dma(4, nf),
            dma(4, nf),
            dma(4, nf),
        ],
        compiler_params=pltpu.CompilerParams(
            collective_id=1, has_side_effects=True, vmem_limit_bytes=40 * MIB
        ),
        cost_estimate=pl.CostEstimate(
            flops=8 * share * full * full, bytes_accessed=60 * MIB, transcendentals=share * full
        ),
        name="nodes",
    )(summed, rows, we, wi, wo, norms)


def solution(mesh):
    in_specs = (
        P("dom", "feat"),
        P(None, "feat"),
        P(None, "feat"),
        P("feat", None),
        P(None, "feat"),
        P("feat", None),
        P("feat"),
        P("feat"),
        P("dom", None),
        P("dom", None),
        P("dom", None),
        P("dom", None),
        P("dom"),
        P("dom", None, None),
    )
    out_specs = P("dom", "feat")
    return jax.shard_map(body, mesh=mesh, in_specs=in_specs, out_specs=out_specs, check_vma=False)
```

```python
import functools

import jax
import jax.numpy as jnp
from jax import lax
from jax.experimental import pallas as pl
from jax.experimental.pallas import tpu as pltpu
from jax.sharding import PartitionSpec as P

TILE = 128
CT = 2
W = 2
MESH = pl.DeviceIdType.MESH
BF = jnp.bfloat16
F32 = jnp.float32
MIB = 1 << 20

epsilon = 1e-05


def swish(v):
    half = 0.5 * v
    return half + half * jnp.tanh(half)


def project_kernel(
    lat_ref,
    ws_hbm,
    wd_hbm,
    st_ref,
    norm_ref,
    we_own,
    wi_own,
    wo_own,
    table_ref,
    recv_ref,
    rows_ref,
    norm_all,
    we_all,
    wi_all,
    wo_all,
    ws_ref,
    wd_ref,
    parts,
    held,
    halo,
    own_sem,
    a1_send,
    a1_recv,
    a2_send,
    a2_recv,
    b_send,
    b_recv,
    c_send,
    c_recv,
    h_send,
    h_recv,
    n_send,
    n_recv,
    near_send,
    near_recv,
    far_send,
    far_recv,
    pass_send,
    pass_recv,
    load_sem,
):
    nf, nodes, width = parts.shape
    nd = lax.axis_size("dom")
    feat = lax.axis_index("feat")
    dom = lax.axis_index("dom")
    rounds, batch = st_ref.shape[1:]
    chunks = a1_send.shape[0]
    step = nodes // chunks
    x, core = feat // 2, feat % 2
    near = x * 2 + (1 - core)
    far = (1 - x) * 2 + core
    offsets = list(range(-W, 0)) + list(range(1, W + 1))
    coarse_at = nodes + rounds * batch * TILE
    coarse_rows = CT * TILE

    barrier = pltpu.get_barrier_semaphore()
    for peer in (near, far):
        pl.semaphore_signal(barrier, inc=1, device_id={"feat": peer}, device_id_type=MESH)
    for k in range(1, nd):
        pl.semaphore_signal(
            barrier, inc=1, device_id={"dom": lax.rem(dom + k, nd)}, device_id_type=MESH
        )
    pl.semaphore_wait(barrier, nd + 1)

    def first(c, peer, send, recv):
        rows = pl.ds(c * step, step)
        return pltpu.make_async_remote_copy(
            src_ref=lat_ref.at[rows],
            dst_ref=parts.at[feat, rows],
            send_sem=send.at[c],
            recv_sem=recv.at[c],
            device_id={"feat": peer},
            device_id_type=MESH,
        )

    to_far = [first(c, far, a2_send, a2_recv) for c in range(chunks)]
    to_near = [first(c, near, a1_send, a1_recv) for c in range(chunks)]
    onward = []
    for c in range(chunks):
        rows = pl.ds(c * step, step)
        onward.append(
            pltpu.make_async_remote_copy(
                src_ref=parts.at[far, rows],
                dst_ref=parts.at[far, rows],
                send_sem=b_send.at[c],
                recv_sem=b_recv.at[c],
                device_id={"feat": near},
                device_id_type=MESH,
            )
        )
    own = pltpu.make_async_copy(lat_ref, parts.at[feat], own_sem)
    loads = [
        pltpu.make_async_copy(src, dst, load_sem.at[i])
        for i, (src, dst) in enumerate(
            (
                (ws_hbm, ws_ref),
                (wd_hbm, wd_ref),
                (we_own, we_all.at[feat]),
                (wi_own, wi_all.at[feat]),
                (wo_own, wo_all.at[feat]),
            )
        )
    ]

    def remote(src, dst, send, recv, i, peer):
        return pltpu.make_async_remote_copy(
            src_ref=src,
            dst_ref=dst,
            send_sem=send.at[i],
            recv_sem=recv.at[i],
            device_id=peer,
            device_id_type=MESH,
        )

    pieces = []
    for src, dst in ((we_own, we_all), (wo_own, wo_all)):
        size = width // 2
        for i in range(2):
            pieces.append((src, dst, pl.ds(i * size, size)))
    weights_near = [
        remote(src, dst.at[feat], near_send, near_recv, i, {"feat": near})
        for i, (src, dst) in enumerate(((we_own, we_all), (wi_own, wi_all), (wo_own, wo_all)))
    ]
    weights_far = [
        remote(src.at[at], dst.at[feat, at], far_send, far_recv, i, {"feat": far})
        for i, (src, dst, at) in enumerate(pieces)
    ]
    weights_pass = [
        remote(dst.at[far, at], dst.at[far, at], pass_send, pass_recv, i, {"feat": near})
        for i, (src, dst, at) in enumerate(pieces)
    ]
    norms = [
        remote(norm_ref, norm_all.at[feat], n_send, n_recv, 0, {"feat": far}),
        remote(norm_ref, norm_all.at[feat], n_send, n_recv, 1, {"feat": near}),
        remote(norm_all.at[far], norm_all.at[far], n_send, n_recv, 2, {"feat": near}),
    ]
    norms[0].start()
    norms[1].start()
    norm_all[feat] = norm_ref[...]
    for c in range(chunks):
        to_far[c].start()
    own.start()
    for c in range(chunks):
        to_near[c].start()
    for load in loads:
        load.start()
    own.wait()
    loads[0].wait()
    loads[1].wait()

    coarse = []
    for k in range(1, nd):
        coarse.append(
            pltpu.make_async_remote_copy(
                src_ref=table_ref.at[pl.ds(0, coarse_rows)],
                dst_ref=table_ref.at[pl.ds(coarse_at + dom * coarse_rows, coarse_rows)],
                send_sem=c_send.at[k],
                recv_sem=c_recv.at[k],
                device_id={"dom": lax.rem(dom + k, nd)},
                device_id_type=MESH,
            )
        )

    def project(c):
        to_near[c].wait_recv()
        onward[c].wait_recv()
        rows = pl.ds(c * step, step)
        lat = jnp.concatenate([parts[f, rows, :] for f in range(nf)], axis=1)
        sent = jnp.dot(lat, ws_ref[...], preferred_element_type=F32).astype(BF)
        tiles = step // TILE
        held[pl.ds(c * tiles, tiles)] = sent.reshape(tiles, TILE, width)
        table_ref[rows, :] = sent
        recv_ref[rows, :] = jnp.dot(lat, wd_ref[...], preferred_element_type=F32).astype(BF)
        if c == 0:
            for copy in coarse:
                copy.start()
            table_ref[pl.ds(coarse_at + dom * coarse_rows, coarse_rows), :] = sent[:coarse_rows]

    for c in range(chunks):
        to_far[c].wait_recv()
        onward[c].start()
        if c == chunks - 2:
            for copy in weights_far:
                copy.start()
        if c > 0:
            project(c - 1)
    project(chunks - 1)

    spread = []
    for r, offset in enumerate(offsets):
        base = nodes + r * batch * TILE
        for b in range(batch):
            tile = st_ref[0, r, b]
            halo[r, pl.ds(b * TILE, TILE), :] = held[tile]
        target = dom - offset
        copy = pltpu.make_async_remote_copy(
            src_ref=halo.at[r],
            dst_ref=table_ref.at[pl.ds(base, batch * TILE)],
            send_sem=h_send.at[r],
            recv_sem=h_recv.at[r],
            device_id={"dom": lax.rem(target + nd, nd)},
            device_id_type=MESH,
        )
        source = dom + offset
        sends = target >= 0 if offset > 0 else target < nd
        gets = source >= 0 if offset < 0 else source < nd
        lacks = source < 0 if offset < 0 else source >= nd
        spread.append((copy, sends, gets))

        @pl.when(sends)
        def _(copy=copy):
            copy.start()

        @pl.when(lacks)
        def _(base=base):
            table_ref[pl.ds(base, batch * TILE), :] = jnp.zeros((batch * TILE, width), BF)

    for copy in weights_near:
        copy.start()
    norms[0].wait_recv()
    norms[2].start()
    share = nodes // nf
    for f in range(nf):
        rows_ref[:, f * width : (f + 1) * width] = parts[f, pl.ds(feat * share, share), :]

    for came, passed in zip(weights_far, weights_pass):
        came.wait_recv()
        passed.start()

    for copy, sends, gets in spread:

        @pl.when(sends)
        def _(copy=copy):
            copy.wait_send()

        @pl.when(gets)
        def _(copy=copy):
            copy.wait_recv()

    for copy in coarse:
        copy.wait_send()
        copy.wait_recv()
    for c in range(chunks):
        to_far[c].wait_send()
        to_near[c].wait_send()
        onward[c].wait_send()
    for copy in weights_near + weights_pass + norms[1:]:
        copy.wait_send()
        copy.wait_recv()
    for copy in weights_far + norms[:1]:
        copy.wait_send()
    for load in loads[2:]:
        load.wait()


UNROLL = 4


def edge_kernel(
    idx_ref,
    dst_tile_ref,
    count_ref,
    off_ref,
    table_hbm,
    recv_hbm,
    out_ref,
    table_ref,
    recv_ref,
    wide,
    acc,
    sems,
    *slots,
):
    rows, width = table_ref.shape
    half = width // 2
    block = 8 * TILE

    loads = []
    for i in range(rows // block):
        at = pl.ds(i * block, block)
        loads.append(pltpu.make_async_copy(table_hbm.at[at], table_ref.at[at], sems.at[i]))
    loads.append(pltpu.make_async_copy(recv_hbm, recv_ref, sems.at[rows // block]))
    for load in loads:
        load.start()
    acc[...] = jnp.zeros_like(acc)
    for i in range(rows // block):
        loads[i].wait()
        part = table_ref[pl.ds(i * block, block), :].astype(F32)
        wide[pl.ds(2 * i * block, block, stride=2), :] = part[:, :half]
        wide[pl.ds(2 * i * block + 1, block, stride=2), :] = part[:, half:]
    loads[-1].wait()
    ids = lax.broadcasted_iota(jnp.int32, (TILE, TILE), 0)
    count = count_ref[0]

    @pl.loop(0, (count + UNROLL - 1) // UNROLL)
    def _(i):
        for u in range(UNROLL):
            e = i * UNROLL + u
            slot = slots[u]
            for n in range(TILE):
                slot[pl.ds(2 * n, 2), :] = wide[pl.ds(idx_ref[e, n], 2), :]
        for u in range(UNROLL):
            e = i * UNROLL + u
            slot = slots[u]
            live = (e < count).astype(F32)
            node = pl.ds(pl.multiple_of(dst_tile_ref[0, e] * TILE, TILE), TILE)
            scatter = (ids == off_ref[pl.ds(e, 1), :]).astype(F32).astype(BF)
            target = lax.dot_general(
                scatter, recv_ref[node, :], (((0,), (0,)), ((), ())), preferred_element_type=F32
            )
            source = jnp.concatenate(
                [slot[pl.ds(0, TILE, stride=2), :], slot[pl.ds(1, TILE, stride=2), :]], axis=1
            )
            message = (swish(source + target) * live).astype(BF)
            acc[node, :] += jnp.dot(scatter, message, preferred_element_type=F32)

    out_ref[...] = acc[...].astype(BF)


def node_kernel(
    summed_ref,
    rows_hbm,
    we_hbm,
    wi_hbm,
    wi_far,
    wo_hbm,
    norm_ref,
    out_ref,
    rows_ref,
    we,
    wi,
    wo,
    taken,
    given,
    load_sem,
    keep_sem,
    in_send,
    in_recv,
    out_send,
    out_recv,
    pass_send,
    pass_recv,
):
    nf, share, width = taken.shape
    full = nf * width
    feat = lax.axis_index("feat")
    chunks = keep_sem.shape[0]
    step = share // chunks

    barrier = pltpu.get_barrier_semaphore()
    for k in range(1, nf):
        pl.semaphore_signal(
            barrier, inc=1, device_id={"feat": lax.rem(feat + k, nf)}, device_id_type=MESH
        )
    x, core = feat // 2, feat % 2
    near = x * 2 + (1 - core)
    far = (1 - x) * 2 + core
    passed = pltpu.make_async_remote_copy(
        src_ref=wi_far,
        dst_ref=wi.at[far],
        send_sem=pass_send.at[0],
        recv_sem=pass_recv.at[0],
        device_id={"feat": near},
        device_id_type=MESH,
    )
    loads = [
        pltpu.make_async_copy(src, dst, load_sem.at[i])
        for i, (src, dst) in enumerate(
            (
                (rows_hbm, rows_ref),
                (wi_hbm.at[feat], wi.at[feat]),
                (wi_hbm.at[near], wi.at[near]),
                (wi_far, wi.at[far]),
                (summed_ref.at[pl.ds(feat * share, share)], taken.at[feat]),
                (we_hbm, we),
                (wo_hbm, wo),
            )
        )
    ]
    pl.semaphore_wait(barrier, nf - 1)

    ins = {}
    for c in range(chunks):
        for k in (2, 1, 3):
            peer = lax.rem(feat + k, nf)
            ins[c, k] = pltpu.make_async_remote_copy(
                src_ref=summed_ref.at[pl.ds(peer * share + c * step, step)],
                dst_ref=taken.at[feat, pl.ds(c * step, step)],
                send_sem=in_send.at[c, k],
                recv_sem=in_recv.at[c, k],
                device_id={"feat": peer},
                device_id_type=MESH,
            )
            ins[c, k].start()
    for load in loads:
        load.start()
    passed.start()
    gain = jnp.concatenate([norm_ref[f, 0:1, :] for f in range(nf)], axis=1)
    bias = jnp.concatenate([norm_ref[f, 1:2, :] for f in range(nf)], axis=1)
    for load in loads[:4]:
        load.wait()
    passed.wait_recv()

    outs = []
    keeps = []
    for c in range(chunks):
        rows = pl.ds(c * step, step)
        lat = rows_ref[rows, :]
        first = [
            jnp.dot(lat, wi[f, :full, :], preferred_element_type=F32) for f in range(nf)
        ]
        for k in (2, 1, 3):
            ins[c, k].wait_recv()
        if c == 0:
            for load in loads[4:]:
                load.wait()
        total = jnp.zeros((step, full), F32)
        for f in range(nf):
            term = jnp.dot(
                taken[f, rows, :], we[f], preferred_element_type=F32
            )
            total = total + term.astype(BF).astype(F32)
        aggregate = total.astype(BF)
        update = jnp.zeros((step, full), F32)
        for f in range(nf):
            pre = first[f] + jnp.dot(aggregate, wi[f, full:, :], preferred_element_type=F32)
            hidden = swish(pre).astype(BF)
            term = jnp.dot(hidden, wo[f], preferred_element_type=F32)
            update = update + term.astype(BF).astype(F32)
        average = jnp.sum(update, axis=1, keepdims=True) / full
        spread = jnp.sum(update * update, axis=1, keepdims=True) / full - average * average
        normed = (update - average) * lax.rsqrt(spread + epsilon) * gain + bias
        result = (lat.astype(F32) + normed).astype(BF)
        for f in range(nf):
            given[f, rows, :] = result[:, f * width : (f + 1) * width]
        place = pl.ds(feat * share + c * step, step)
        for k in (2, 1, 3):
            peer = lax.rem(feat + k, nf)
            copy = pltpu.make_async_remote_copy(
                src_ref=given.at[peer, rows],
                dst_ref=out_ref.at[place],
                send_sem=out_send.at[c, k],
                recv_sem=out_recv.at[c, k],
                device_id={"feat": peer},
                device_id_type=MESH,
            )
            copy.start()
            outs.append(copy)
        keep = pltpu.make_async_copy(given.at[feat, rows], out_ref.at[place], keep_sem.at[c])
        keep.start()
        keeps.append(keep)
    passed.wait_send()
    for keep in keeps:
        keep.wait()
    for copy in outs:
        copy.wait_send()
        copy.wait_recv()
    for copy in ins.values():
        copy.wait_send()


def vmem():
    return pl.BlockSpec(memory_space=pltpu.VMEM)


def smem():
    return pl.BlockSpec(memory_space=pltpu.SMEM)


def hbm():
    return pl.BlockSpec(memory_space=pl.ANY)


def dma(*shape):
    return pltpu.SemaphoreType.DMA(shape)


def body(
    latents,
    w_src,
    w_dst,
    w_edge_out,
    w_node_in,
    w_node_out,
    norm_gain,
    norm_bias,
    src_tile,
    dst_tile,
    src_off,
    dst_off,
    edge_count,
    send_tiles,
):
    nodes, width = latents.shape
    full = w_src.shape[0]
    nf = lax.axis_size("feat")
    nd = lax.axis_size("dom")
    rounds, batch = send_tiles.shape[1:]
    share = nodes // nf
    table_rows = nodes + rounds * batch * TILE + nd * CT * TILE
    edge_tiles = src_tile.shape[0]
    chunks = 8

    norm = jnp.stack([norm_gain, norm_bias])

    table, received, rows, norms, we, wi, wo = pl.pallas_call(
        project_kernel,
        out_shape=(
            jax.ShapeDtypeStruct((table_rows, width), BF),
            jax.ShapeDtypeStruct((nodes, width), BF),
            jax.ShapeDtypeStruct((share, full), BF),
            jax.ShapeDtypeStruct((nf, 2, width), F32),
            jax.ShapeDtypeStruct((nf, width, full), BF),
            jax.ShapeDtypeStruct((nf, 2 * full, width), BF),
            jax.ShapeDtypeStruct((nf, width, full), BF),
        ),
        in_specs=[hbm(), hbm(), hbm(), smem(), vmem(), hbm(), hbm(), hbm()],
        out_specs=(vmem(), vmem(), vmem(), vmem(), hbm(), hbm(), hbm()),
        scratch_shapes=[
            pltpu.VMEM((full, width), BF),
            pltpu.VMEM((full, width), BF),
            pltpu.VMEM((nf, nodes, width), BF),
            pltpu.VMEM((nodes // TILE, TILE, width), BF),
            pltpu.VMEM((rounds, batch * TILE, width), BF),
            pltpu.SemaphoreType.DMA,
            *[dma(chunks) for _ in range(6)],
            dma(nd),
            dma(nd),
            dma(rounds),
            dma(rounds),
            dma(3),
            dma(3),
            dma(3),
            dma(3),
            dma(4),
            dma(4),
            dma(4),
            dma(4),
            dma(5),
        ],
        compiler_params=pltpu.CompilerParams(
            collective_id=0, has_side_effects=True, vmem_limit_bytes=62 * MIB
        ),
        cost_estimate=pl.CostEstimate(
            flops=4 * nodes * full * width, bytes_accessed=100 * MIB, transcendentals=0
        ),
        name="project",
    )(latents, w_src, w_dst, send_tiles, norm, w_edge_out, w_node_in, w_node_out)

    crossing, norms = lax.optimization_barrier((w_node_in, norms))
    wi_far = lax.ppermute(crossing, "feat", [(0, 2), (2, 0), (1, 3), (3, 1)])

    index = (src_tile * TILE + src_off) * 2
    summed = pl.pallas_call(
        edge_kernel,
        out_shape=jax.ShapeDtypeStruct((nodes, width), BF),
        in_specs=[smem(), smem(), smem(), vmem(), hbm(), hbm()],
        out_specs=vmem(),
        scratch_shapes=[
            pltpu.VMEM((table_rows, width), BF),
            pltpu.VMEM((nodes, width), BF),
            pltpu.VMEM((2 * table_rows, width // 2), F32),
            pltpu.VMEM((nodes, width), F32),
            dma(table_rows // (8 * TILE) + 1),
            *[pltpu.VMEM((2 * TILE, width // 2), F32) for _ in range(UNROLL)],
        ],
        compiler_params=pltpu.CompilerParams(vmem_limit_bytes=62 * MIB),
        cost_estimate=pl.CostEstimate(
            flops=4 * edge_tiles * TILE * TILE * width,
            bytes_accessed=100 * MIB,
            transcendentals=edge_tiles * TILE * width,
        ),
        name="edges",
    )(index, dst_tile, edge_count, dst_off, table, received)

    return pl.pallas_call(
        node_kernel,
        out_shape=jax.ShapeDtypeStruct((nodes, width), BF),
        in_specs=[hbm(), hbm(), hbm(), hbm(), hbm(), hbm(), vmem()],
        out_specs=hbm(),
        scratch_shapes=[
            pltpu.VMEM((share, full), BF),
            pltpu.VMEM((nf, width, full), BF),
            pltpu.VMEM((nf, 2 * full, width), BF),
            pltpu.VMEM((nf, width, full), BF),
            pltpu.VMEM((nf, share, width), BF),
            pltpu.VMEM((nf, share, width), BF),
            dma(7),
            dma(4),
            dma(4, nf),
            dma(4, nf),
            dma(4, nf),
            dma(4, nf),
            dma(1),
            dma(1),
        ],
        compiler_params=pltpu.CompilerParams(
            collective_id=1, has_side_effects=True, vmem_limit_bytes=62 * MIB
        ),
        cost_estimate=pl.CostEstimate(
            flops=8 * share * full * full, bytes_accessed=60 * MIB, transcendentals=share * full
        ),
        name="nodes",
    )(summed, rows, we, wi, wi_far, wo, norms)


def solution(mesh):
    in_specs = (
        P("dom", "feat"),
        P(None, "feat"),
        P(None, "feat"),
        P("feat", None),
        P(None, "feat"),
        P("feat", None),
        P("feat"),
        P("feat"),
        P("dom", None),
        P("dom", None),
        P("dom", None),
        P("dom", None),
        P("dom"),
        P("dom", None, None),
    )
    out_specs = P("dom", "feat")
    return jax.shard_map(body, mesh=mesh, in_specs=in_specs, out_specs=out_specs, check_vma=False)
```

```python
import functools

import jax
import jax.numpy as jnp
from jax import lax
from jax.experimental import pallas as pl
from jax.experimental.pallas import tpu as pltpu
from jax.sharding import PartitionSpec as P

TILE = 128
CT = 2
W = 2
MESH = pl.DeviceIdType.MESH
BF = jnp.bfloat16
F32 = jnp.float32
MIB = 1 << 20

epsilon = 1e-05


def swish(v):
    half = 0.5 * v
    return half + half * jnp.tanh(half)


def project_kernel(
    lat_ref,
    ws_hbm,
    wd_hbm,
    st_ref,
    norm_ref,
    wi_own,
    table_ref,
    recv_ref,
    rows_ref,
    norm_all,
    wi_all,
    ws_ref,
    wd_ref,
    parts,
    held,
    halo,
    own_sem,
    a1_send,
    a1_recv,
    a2_send,
    a2_recv,
    b_send,
    b_recv,
    c_send,
    c_recv,
    h_send,
    h_recv,
    n_send,
    n_recv,
    near_send,
    near_recv,
    load_sem,
):
    nf, nodes, width = parts.shape
    nd = lax.axis_size("dom")
    feat = lax.axis_index("feat")
    dom = lax.axis_index("dom")
    rounds, batch = st_ref.shape[1:]
    chunks = a1_send.shape[0]
    step = nodes // chunks
    x, core = feat // 2, feat % 2
    near = x * 2 + (1 - core)
    far = (1 - x) * 2 + core
    offsets = list(range(-W, 0)) + list(range(1, W + 1))
    coarse_at = nodes + rounds * batch * TILE
    coarse_rows = CT * TILE

    barrier = pltpu.get_barrier_semaphore()
    for peer in (near, far):
        pl.semaphore_signal(barrier, inc=1, device_id={"feat": peer}, device_id_type=MESH)
    for k in range(1, nd):
        pl.semaphore_signal(
            barrier, inc=1, device_id={"dom": lax.rem(dom + k, nd)}, device_id_type=MESH
        )
    pl.semaphore_wait(barrier, nd + 1)

    def first(c, peer, send, recv):
        rows = pl.ds(c * step, step)
        return pltpu.make_async_remote_copy(
            src_ref=lat_ref.at[rows],
            dst_ref=parts.at[feat, rows],
            send_sem=send.at[c],
            recv_sem=recv.at[c],
            device_id={"feat": peer},
            device_id_type=MESH,
        )

    to_far = [first(c, far, a2_send, a2_recv) for c in range(chunks)]
    to_near = [first(c, near, a1_send, a1_recv) for c in range(chunks)]
    onward = []
    for c in range(chunks):
        rows = pl.ds(c * step, step)
        onward.append(
            pltpu.make_async_remote_copy(
                src_ref=parts.at[far, rows],
                dst_ref=parts.at[far, rows],
                send_sem=b_send.at[c],
                recv_sem=b_recv.at[c],
                device_id={"feat": near},
                device_id_type=MESH,
            )
        )
    own = pltpu.make_async_copy(lat_ref, parts.at[feat], own_sem)
    loads = [
        pltpu.make_async_copy(src, dst, load_sem.at[i])
        for i, (src, dst) in enumerate(
            (
                (ws_hbm, ws_ref),
                (wd_hbm, wd_ref),
                (wi_own, wi_all.at[feat]),
            )
        )
    ]

    def remote(src, dst, send, recv, i, peer):
        return pltpu.make_async_remote_copy(
            src_ref=src,
            dst_ref=dst,
            send_sem=send.at[i],
            recv_sem=recv.at[i],
            device_id=peer,
            device_id_type=MESH,
        )

    weights_near = remote(wi_own, wi_all.at[feat], near_send, near_recv, 0, {"feat": near})
    norms = [
        remote(norm_ref, norm_all.at[feat], n_send, n_recv, 0, {"feat": far}),
        remote(norm_ref, norm_all.at[feat], n_send, n_recv, 1, {"feat": near}),
        remote(norm_all.at[far], norm_all.at[far], n_send, n_recv, 2, {"feat": near}),
    ]
    norms[0].start()
    norms[1].start()
    norm_all[feat] = norm_ref[...]
    for c in range(chunks):
        to_far[c].start()
    own.start()
    for c in range(chunks):
        to_near[c].start()
    for load in loads:
        load.start()
    own.wait()
    loads[0].wait()
    loads[1].wait()

    coarse = []
    for k in range(1, nd):
        coarse.append(
            pltpu.make_async_remote_copy(
                src_ref=table_ref.at[pl.ds(0, coarse_rows)],
                dst_ref=table_ref.at[pl.ds(coarse_at + dom * coarse_rows, coarse_rows)],
                send_sem=c_send.at[k],
                recv_sem=c_recv.at[k],
                device_id={"dom": lax.rem(dom + k, nd)},
                device_id_type=MESH,
            )
        )

    def project(c):
        to_near[c].wait_recv()
        onward[c].wait_recv()
        rows = pl.ds(c * step, step)
        lat = jnp.concatenate([parts[f, rows, :] for f in range(nf)], axis=1)
        sent = jnp.dot(lat, ws_ref[...], preferred_element_type=F32).astype(BF)
        tiles = step // TILE
        held[pl.ds(c * tiles, tiles)] = sent.reshape(tiles, TILE, width)
        table_ref[rows, :] = sent
        recv_ref[rows, :] = jnp.dot(lat, wd_ref[...], preferred_element_type=F32).astype(BF)
        if c == 0:
            for copy in coarse:
                copy.start()
            table_ref[pl.ds(coarse_at + dom * coarse_rows, coarse_rows), :] = sent[:coarse_rows]

    for c in range(chunks):
        to_far[c].wait_recv()
        onward[c].start()
        if c > 0:
            project(c - 1)
    project(chunks - 1)

    spread = []
    for r, offset in enumerate(offsets):
        base = nodes + r * batch * TILE
        for b in range(batch):
            tile = st_ref[0, r, b]
            halo[r, pl.ds(b * TILE, TILE), :] = held[tile]
        target = dom - offset
        copy = pltpu.make_async_remote_copy(
            src_ref=halo.at[r],
            dst_ref=table_ref.at[pl.ds(base, batch * TILE)],
            send_sem=h_send.at[r],
            recv_sem=h_recv.at[r],
            device_id={"dom": lax.rem(target + nd, nd)},
            device_id_type=MESH,
        )
        source = dom + offset
        sends = target >= 0 if offset > 0 else target < nd
        gets = source >= 0 if offset < 0 else source < nd
        lacks = source < 0 if offset < 0 else source >= nd
        spread.append((copy, sends, gets))

        @pl.when(sends)
        def _(copy=copy):
            copy.start()

        @pl.when(lacks)
        def _(base=base):
            table_ref[pl.ds(base, batch * TILE), :] = jnp.zeros((batch * TILE, width), BF)

    weights_near.start()
    norms[0].wait_recv()
    norms[2].start()
    share = nodes // nf
    for f in range(nf):
        rows_ref[:, f * width : (f + 1) * width] = parts[f, pl.ds(feat * share, share), :]

    for copy, sends, gets in spread:

        @pl.when(sends)
        def _(copy=copy):
            copy.wait_send()

        @pl.when(gets)
        def _(copy=copy):
            copy.wait_recv()

    for copy in coarse:
        copy.wait_send()
        copy.wait_recv()
    for c in range(chunks):
        to_far[c].wait_send()
        to_near[c].wait_send()
        onward[c].wait_send()
    for copy in [weights_near] + norms[1:]:
        copy.wait_send()
        copy.wait_recv()
    norms[0].wait_send()
    for load in loads[2:]:
        load.wait()


UNROLL = 4


def edge_kernel(
    idx_ref,
    dst_tile_ref,
    count_ref,
    off_ref,
    table_hbm,
    recv_hbm,
    out_ref,
    table_ref,
    recv_ref,
    wide,
    acc,
    sems,
    *slots,
):
    rows, width = table_ref.shape
    half = width // 2
    block = 8 * TILE

    loads = []
    for i in range(rows // block):
        at = pl.ds(i * block, block)
        loads.append(pltpu.make_async_copy(table_hbm.at[at], table_ref.at[at], sems.at[i]))
    loads.append(pltpu.make_async_copy(recv_hbm, recv_ref, sems.at[rows // block]))
    for load in loads:
        load.start()
    acc[...] = jnp.zeros_like(acc)
    for i in range(rows // block):
        loads[i].wait()
        part = table_ref[pl.ds(i * block, block), :].astype(F32)
        wide[pl.ds(2 * i * block, block, stride=2), :] = part[:, :half]
        wide[pl.ds(2 * i * block + 1, block, stride=2), :] = part[:, half:]
    loads[-1].wait()
    ids = lax.broadcasted_iota(jnp.int32, (TILE, TILE), 0)
    count = count_ref[0]

    @pl.loop(0, (count + UNROLL - 1) // UNROLL)
    def _(i):
        for u in range(UNROLL):
            e = i * UNROLL + u
            slot = slots[u]
            for n in range(TILE):
                slot[pl.ds(2 * n, 2), :] = wide[pl.ds(idx_ref[e, n], 2), :]
        for u in range(UNROLL):
            e = i * UNROLL + u
            slot = slots[u]
            live = (e < count).astype(F32)
            node = pl.ds(pl.multiple_of(dst_tile_ref[0, e] * TILE, TILE), TILE)
            scatter = (ids == off_ref[pl.ds(e, 1), :]).astype(F32).astype(BF)
            target = lax.dot_general(
                scatter, recv_ref[node, :], (((0,), (0,)), ((), ())), preferred_element_type=F32
            )
            source = jnp.concatenate(
                [slot[pl.ds(0, TILE, stride=2), :], slot[pl.ds(1, TILE, stride=2), :]], axis=1
            )
            message = (swish(source + target) * live).astype(BF)
            acc[node, :] += jnp.dot(scatter, message, preferred_element_type=F32)

    out_ref[...] = acc[...].astype(BF)


def node_kernel(
    summed_ref,
    rows_hbm,
    we_hbm,
    wi_hbm,
    wi_far,
    wo_hbm,
    norm_ref,
    out_ref,
    rows_ref,
    we,
    wi,
    wo,
    taken,
    given,
    load_sem,
    keep_sem,
    in_send,
    in_recv,
    out_send,
    out_recv,
    pass_send,
    pass_recv,
):
    nf, share, width = taken.shape
    full = nf * width
    feat = lax.axis_index("feat")
    chunks = keep_sem.shape[0]
    step = share // chunks

    barrier = pltpu.get_barrier_semaphore()
    for k in range(1, nf):
        pl.semaphore_signal(
            barrier, inc=1, device_id={"feat": lax.rem(feat + k, nf)}, device_id_type=MESH
        )
    x, core = feat // 2, feat % 2
    near = x * 2 + (1 - core)
    far = (1 - x) * 2 + core
    passed = pltpu.make_async_remote_copy(
        src_ref=wi_far,
        dst_ref=wi.at[far],
        send_sem=pass_send.at[0],
        recv_sem=pass_recv.at[0],
        device_id={"feat": near},
        device_id_type=MESH,
    )
    loads = [
        pltpu.make_async_copy(src, dst, load_sem.at[i])
        for i, (src, dst) in enumerate(
            (
                (rows_hbm, rows_ref),
                (wi_hbm.at[feat], wi.at[feat]),
                (wi_hbm.at[near], wi.at[near]),
                (wi_far, wi.at[far]),
                (summed_ref.at[pl.ds(feat * share, share)], taken.at[feat]),
                (we_hbm, we),
                (wo_hbm, wo),
            )
        )
    ]
    pl.semaphore_wait(barrier, nf - 1)

    ins = {}
    for c in range(chunks):
        for k in (2, 1, 3):
            peer = lax.rem(feat + k, nf)
            ins[c, k] = pltpu.make_async_remote_copy(
                src_ref=summed_ref.at[pl.ds(peer * share + c * step, step)],
                dst_ref=taken.at[feat, pl.ds(c * step, step)],
                send_sem=in_send.at[c, k],
                recv_sem=in_recv.at[c, k],
                device_id={"feat": peer},
                device_id_type=MESH,
            )
            ins[c, k].start()
    for load in loads:
        load.start()
    passed.start()
    gain = jnp.concatenate([norm_ref[f, 0:1, :] for f in range(nf)], axis=1)
    bias = jnp.concatenate([norm_ref[f, 1:2, :] for f in range(nf)], axis=1)
    for load in loads[:4]:
        load.wait()
    passed.wait_recv()

    outs = []
    keeps = []
    for c in range(chunks):
        rows = pl.ds(c * step, step)
        lat = rows_ref[rows, :]
        first = [
            jnp.dot(lat, wi[f, :full, :], preferred_element_type=F32) for f in range(nf)
        ]
        for k in (2, 1, 3):
            ins[c, k].wait_recv()
        if c == 0:
            for load in loads[4:]:
                load.wait()
        total = jnp.zeros((step, full), F32)
        for f in range(nf):
            term = jnp.dot(
                taken[f, rows, :], we[f], preferred_element_type=F32
            )
            total = total + term.astype(BF).astype(F32)
        aggregate = total.astype(BF)
        update = jnp.zeros((step, full), F32)
        for f in range(nf):
            pre = first[f] + jnp.dot(aggregate, wi[f, full:, :], preferred_element_type=F32)
            hidden = swish(pre).astype(BF)
            term = jnp.dot(hidden, wo[f], preferred_element_type=F32)
            update = update + term.astype(BF).astype(F32)
        average = jnp.sum(update, axis=1, keepdims=True) / full
        spread = jnp.sum(update * update, axis=1, keepdims=True) / full - average * average
        normed = (update - average) * lax.rsqrt(spread + epsilon) * gain + bias
        result = (lat.astype(F32) + normed).astype(BF)
        for f in range(nf):
            given[f, rows, :] = result[:, f * width : (f + 1) * width]
        place = pl.ds(feat * share + c * step, step)
        for k in (2, 1, 3):
            peer = lax.rem(feat + k, nf)
            copy = pltpu.make_async_remote_copy(
                src_ref=given.at[peer, rows],
                dst_ref=out_ref.at[place],
                send_sem=out_send.at[c, k],
                recv_sem=out_recv.at[c, k],
                device_id={"feat": peer},
                device_id_type=MESH,
            )
            copy.start()
            outs.append(copy)
        keep = pltpu.make_async_copy(given.at[feat, rows], out_ref.at[place], keep_sem.at[c])
        keep.start()
        keeps.append(keep)
    passed.wait_send()
    for keep in keeps:
        keep.wait()
    for copy in outs:
        copy.wait_send()
        copy.wait_recv()
    for copy in ins.values():
        copy.wait_send()


def vmem():
    return pl.BlockSpec(memory_space=pltpu.VMEM)


def smem():
    return pl.BlockSpec(memory_space=pltpu.SMEM)


def hbm():
    return pl.BlockSpec(memory_space=pl.ANY)


def dma(*shape):
    return pltpu.SemaphoreType.DMA(shape)


def body(
    latents,
    w_src,
    w_dst,
    w_edge_out,
    w_node_in,
    w_node_out,
    norm_gain,
    norm_bias,
    src_tile,
    dst_tile,
    src_off,
    dst_off,
    edge_count,
    send_tiles,
):
    nodes, width = latents.shape
    full = w_src.shape[0]
    nf = lax.axis_size("feat")
    nd = lax.axis_size("dom")
    rounds, batch = send_tiles.shape[1:]
    share = nodes // nf
    table_rows = nodes + rounds * batch * TILE + nd * CT * TILE
    edge_tiles = src_tile.shape[0]
    chunks = 8

    we = lax.all_gather(w_edge_out, "feat", axis=0)
    wo = lax.all_gather(w_node_out, "feat", axis=0)
    norm = jnp.stack([norm_gain, norm_bias])

    table, received, rows, norms, wi = pl.pallas_call(
        project_kernel,
        out_shape=(
            jax.ShapeDtypeStruct((table_rows, width), BF),
            jax.ShapeDtypeStruct((nodes, width), BF),
            jax.ShapeDtypeStruct((share, full), BF),
            jax.ShapeDtypeStruct((nf, 2, width), F32),
            jax.ShapeDtypeStruct((nf, 2 * full, width), BF),
        ),
        in_specs=[hbm(), hbm(), hbm(), smem(), vmem(), hbm()],
        out_specs=(vmem(), vmem(), vmem(), vmem(), hbm()),
        scratch_shapes=[
            pltpu.VMEM((full, width), BF),
            pltpu.VMEM((full, width), BF),
            pltpu.VMEM((nf, nodes, width), BF),
            pltpu.VMEM((nodes // TILE, TILE, width), BF),
            pltpu.VMEM((rounds, batch * TILE, width), BF),
            pltpu.SemaphoreType.DMA,
            *[dma(chunks) for _ in range(6)],
            dma(nd),
            dma(nd),
            dma(rounds),
            dma(rounds),
            dma(3),
            dma(3),
            dma(1),
            dma(1),
            dma(3),
        ],
        compiler_params=pltpu.CompilerParams(
            collective_id=0, has_side_effects=True, vmem_limit_bytes=62 * MIB
        ),
        cost_estimate=pl.CostEstimate(
            flops=4 * nodes * full * width, bytes_accessed=100 * MIB, transcendentals=0
        ),
        name="project",
    )(latents, w_src, w_dst, send_tiles, norm, w_node_in)

    crossing, norms = lax.optimization_barrier((w_node_in, norms))
    wi_far = lax.ppermute(crossing, "feat", [(0, 2), (2, 0), (1, 3), (3, 1)])

    index = (src_tile * TILE + src_off) * 2
    summed = pl.pallas_call(
        edge_kernel,
        out_shape=jax.ShapeDtypeStruct((nodes, width), BF),
        in_specs=[smem(), smem(), smem(), vmem(), hbm(), hbm()],
        out_specs=vmem(),
        scratch_shapes=[
            pltpu.VMEM((table_rows, width), BF),
            pltpu.VMEM((nodes, width), BF),
            pltpu.VMEM((2 * table_rows, width // 2), F32),
            pltpu.VMEM((nodes, width), F32),
            dma(table_rows // (8 * TILE) + 1),
            *[pltpu.VMEM((2 * TILE, width // 2), F32) for _ in range(UNROLL)],
        ],
        compiler_params=pltpu.CompilerParams(vmem_limit_bytes=62 * MIB),
        cost_estimate=pl.CostEstimate(
            flops=4 * edge_tiles * TILE * TILE * width,
            bytes_accessed=100 * MIB,
            transcendentals=edge_tiles * TILE * width,
        ),
        name="edges",
    )(index, dst_tile, edge_count, dst_off, table, received)

    return pl.pallas_call(
        node_kernel,
        out_shape=jax.ShapeDtypeStruct((nodes, width), BF),
        in_specs=[hbm(), hbm(), hbm(), hbm(), hbm(), hbm(), vmem()],
        out_specs=hbm(),
        scratch_shapes=[
            pltpu.VMEM((share, full), BF),
            pltpu.VMEM((nf, width, full), BF),
            pltpu.VMEM((nf, 2 * full, width), BF),
            pltpu.VMEM((nf, width, full), BF),
            pltpu.VMEM((nf, share, width), BF),
            pltpu.VMEM((nf, share, width), BF),
            dma(7),
            dma(4),
            dma(4, nf),
            dma(4, nf),
            dma(4, nf),
            dma(4, nf),
            dma(1),
            dma(1),
        ],
        compiler_params=pltpu.CompilerParams(
            collective_id=1, has_side_effects=True, vmem_limit_bytes=62 * MIB
        ),
        cost_estimate=pl.CostEstimate(
            flops=8 * share * full * full, bytes_accessed=60 * MIB, transcendentals=share * full
        ),
        name="nodes",
    )(summed, rows, we, wi, wi_far, wo, norms)


def solution(mesh):
    in_specs = (
        P("dom", "feat"),
        P(None, "feat"),
        P(None, "feat"),
        P("feat", None),
        P(None, "feat"),
        P("feat", None),
        P("feat"),
        P("feat"),
        P("dom", None),
        P("dom", None),
        P("dom", None),
        P("dom", None),
        P("dom"),
        P("dom", None, None),
    )
    out_specs = P("dom", "feat")
    return jax.shard_map(body, mesh=mesh, in_specs=in_specs, out_specs=out_specs, check_vma=False)
```
